32 devices in a mesh: groups: 2 (over y), acq: 4 (over z), az: 2 (over x), rg: 2 (over core).
Axes of the slice: x: 2, y: 2, z: 4, core: 2. Of those that a mesh axis runs over, the one named last changes fastest.
Arguments:
- slc_tiles: bfloat16 [4, 2, 256, 256], P('acq', None, ('groups', 'az'), 'rg'), parts along dimension 2, may hold values from -60 to 60, as said below
- pair_list: int32 [64, 2], replicated, may hold values from 0 to 3, as said below
- assignment: int32 [64], replicated, may hold values from 0 to 63, each once
Outputs:
- filtered: float32 [64, 2, 256, 256], P('acq', None, ('groups', 'az'), 'rg'), parts along dimension 2
- coherence: float32 [64, 256, 256], P('acq', ('groups', 'az'), 'rg'), parts along dimension 1
The draws below stay inside these ranges and needn't reach their ends.
There are 2 independent parts, one for each index of `groups`. The reference program is written for one: setup_inputs(seed, part) draws one part's arguments, and reference() takes and returns one part's arrays. A program takes and returns all parts, laid end to end along the dimension named above; an argument that names none is the same for every part. Nothing has to cross between parts.
Inputs may be any that keep to these rules, and one draw needn't show every extreme that they name: `slc_tiles`: complex images of one scene with a per-acquisition phase ramp. `pair_list`: each row holds a reference index and a larger secondary index.
All inputs are finite; a program needn't handle non-finite values.
Results may differ from the reference program's by a relative error of at most 0.0003.
Values may be sent and summed in bfloat16 or wider, within the bound.
No kernel may reach another device: no remote copies, remote signals or barrier semaphores. Data moves between devices by JAX's collectives and lax.ppermute only.
A program may use at most 64 MiB of HBM per device.

```python
import math
import jax
import jax.numpy as jnp
from jax import lax

PATCH = 32
LOOKS = 5
ACQ = 4
PAIRS = 64
NH = 128
NW = 256


def draw_slc_tiles(key, part):
    key = jax.random.fold_in(key, 11)
    keys = jax.random.split(key, 8)
    common = jax.random.normal(keys[0], (2, NH, NW), jnp.float32)
    private = jax.random.normal(keys[1], (ACQ, 2, NH, NW), jnp.float32)
    likeness = jax.random.uniform(keys[2], (NH, NW), jnp.float32, 0.2, 0.95)
    amplitude = jnp.exp(jax.random.uniform(keys[3], (NH, NW), jnp.float32, -2.5, 1.0))
    side = PATCH // 2
    block_rows = NH // side
    block_cols = NW // side
    marks = jax.random.randint(keys[5], (block_rows, block_cols), 0, 20) < 3
    forced = jax.random.randint(keys[6], (), 0, block_rows * block_cols)
    numbers = jnp.arange(block_rows * block_cols, dtype=jnp.int32).reshape(block_rows, block_cols)
    shadow = marks | (numbers == forced)
    shadow = jnp.repeat(jnp.repeat(shadow, side, axis=0), side, axis=1)
    faint = jnp.exp(jax.random.uniform(keys[7], (NH, NW), jnp.float32, -7.5, -6.0))
    amplitude = jnp.where(shadow, faint, amplitude)
    slopes = jax.random.uniform(keys[4], (ACQ, 2), jnp.float32, -0.3, 0.3)
    row_pos = jnp.arange(NH, dtype=jnp.float32)[None, :, None]
    col_pos = jnp.arange(NW, dtype=jnp.float32)[None, None, :]
    phase = slopes[:, 0, None, None] * row_pos + slopes[:, 1, None, None] * col_pos
    mixed = likeness * common[None] + jnp.sqrt(1.0 - likeness * likeness) * private
    cosine = jnp.cos(phase)
    sine = jnp.sin(phase)
    real_part = amplitude * (mixed[:, 0] * cosine - mixed[:, 1] * sine)
    imag_part = amplitude * (mixed[:, 0] * sine + mixed[:, 1] * cosine)
    return jnp.stack([real_part, imag_part], axis=1).astype(jnp.bfloat16)


def draw_pair_list(key, part):
    key = jax.random.fold_in(key, 5)
    key_first, key_gap = jax.random.split(key)
    first = jax.random.randint(key_first, (PAIRS,), 0, ACQ - 1)
    first = first.at[0].set(0).at[1].set(ACQ - 2)
    spread = jax.random.randint(key_gap, (PAIRS,), 0, 6)
    second = first + 1 + spread % (ACQ - 1 - first)
    return jnp.stack([first, second], axis=1).astype(jnp.int32)


def setup_inputs(seed: int = 0, part: int = 0) -> dict:
    splits = jax.random.split(jax.random.key(seed), 4)
    part_splits = jax.random.split(jax.random.fold_in(splits[3], part), 4)
    return {
        "slc_tiles": draw_slc_tiles(jax.random.fold_in(jax.random.fold_in(splits[3], part), 71), part),
        "pair_list": draw_pair_list(jax.random.fold_in(splits[3], 71), part),
        "assignment": jax.random.permutation(splits[2], PAIRS).astype(jnp.int32),
    }


spectral_power = 0.5
floor_value = 1.0
tiny_level = 1e-06
highest = lax.Precision.HIGHEST

def dft_table(length):
    indices = jnp.arange(length, dtype=jnp.int32)
    product = indices[:, None] * indices[None, :] % length
    angle = product.astype(jnp.float32) * (-2.0 * math.pi / length)
    return (jnp.cos(angle), jnp.sin(angle))

def complex_product(form, left_real, left_imag, right_real, right_imag):
    real_part = jnp.einsum(form, left_real, right_real, precision=highest) - jnp.einsum(form, left_imag, right_imag, precision=highest)
    imag_part = jnp.einsum(form, left_real, right_imag, precision=highest) + jnp.einsum(form, left_imag, right_real, precision=highest)
    return (real_part, imag_part)

def goldstein(field):
    length = PATCH
    stride = length // 2
    table_real, table_imag = dft_table(length)
    row_blocks = field.shape[1] // stride
    col_blocks = field.shape[2] // stride
    blocks = field.reshape(2, row_blocks, stride, field.shape[2])
    strips = jnp.concatenate([blocks[:, :-1], blocks[:, 1:]], axis=2)
    spec_real, spec_imag = complex_product('ui,kiw->kuw', table_real, table_imag, strips[0], strips[1])
    patch_rows = row_blocks - 1
    patch_cols = col_blocks - 1
    spec_real = spec_real.reshape(patch_rows, length, col_blocks, stride)
    spec_imag = spec_imag.reshape(patch_rows, length, col_blocks, stride)
    spec_real = jnp.concatenate([spec_real[:, :, :-1], spec_real[:, :, 1:]], axis=3)
    spec_imag = jnp.concatenate([spec_imag[:, :, :-1], spec_imag[:, :, 1:]], axis=3)
    spec_real, spec_imag = complex_product('kucj,vj->kucv', spec_real, spec_imag, table_real, table_imag)
    energy = spec_real * spec_real + spec_imag * spec_imag
    response = jnp.power(energy, 0.5 * spectral_power)
    level = lax.optimization_barrier(jnp.mean(response, axis=(1, 3), keepdims=True)) + tiny_level
    weight = response / level
    back_real, back_imag = complex_product('kucv,jv->kucj', spec_real * weight, spec_imag * weight, table_real, -table_imag)
    back_real, back_imag = complex_product('kucj,iu->kicj', back_real, back_imag, table_real, -table_imag)
    position = jnp.arange(length, dtype=jnp.float32)
    window = 1.0 - jnp.abs(position - (length - 1) / 2.0) / stride
    taper = window[None, :, None, None] * window[None, None, None, :] / (length * length)
    results = []
    for part_field in (back_real * taper, back_imag * taper):
        joined = part_field[..., :stride][:, :, 1:] + part_field[..., stride:][:, :, :-1]
        joined = joined.reshape(patch_rows, length, (patch_cols - 1) * stride)
        joined = joined[:, :stride][1:] + joined[:, stride:][:-1]
        results.append(joined.reshape((patch_rows - 1) * stride, (patch_cols - 1) * stride))
    return jnp.stack(results)

def interfere(tile_one, tile_two):
    one_real = tile_one[..., 0, :, :]
    one_imag = tile_one[..., 1, :, :]
    two_real = tile_two[..., 0, :, :]
    two_imag = tile_two[..., 1, :, :]
    cross_real = one_real * two_real + one_imag * two_imag
    cross_imag = one_imag * two_real - one_real * two_imag
    power_one = one_real * one_real + one_imag * one_imag
    power_two = two_real * two_real + two_imag * two_imag
    return jnp.stack([cross_real, cross_imag, power_one, power_two], axis=-3)

def box_sum(field, reach):
    extent_rows = field.shape[-2] - 2 * reach
    extent_cols = field.shape[-1] - 2 * reach
    along_rows = field[..., 0:extent_rows, :]
    for shift in range(1, 2 * reach + 1):
        along_rows = along_rows + field[..., shift:shift + extent_rows, :]
    total = along_rows[..., 0:extent_cols]
    for shift in range(1, 2 * reach + 1):
        total = total + along_rows[..., shift:shift + extent_cols]
    return total

def coherence_of(summed):
    scale = 1.0 / jnp.sqrt(jnp.maximum(summed[..., 2, :, :] * summed[..., 3, :, :], floor_value))
    return jnp.stack([summed[..., 0, :, :] * scale, summed[..., 1, :, :] * scale], axis=-3)

def reference(slc_tiles, pair_list, assignment):
    reach = LOOKS // 2
    stride = PATCH // 2

    def one_slot(pair_id):
        first = lax.dynamic_index_in_dim(pair_list[:, 0], pair_id, 0, keepdims=False)
        second = lax.dynamic_index_in_dim(pair_list[:, 1], pair_id, 0, keepdims=False)
        tile_one = lax.dynamic_index_in_dim(slc_tiles, first, 0, keepdims=False).astype(jnp.float32)
        tile_two = lax.dynamic_index_in_dim(slc_tiles, second, 0, keepdims=False).astype(jnp.float32)
        fields = interfere(tile_one, tile_two)
        padded = jnp.pad(fields, ((0, 0), (reach, reach), (reach, reach)))
        coherent = coherence_of(box_sum(padded, reach))
        magnitude = jnp.sqrt(coherent[0] * coherent[0] + coherent[1] * coherent[1])
        smoothed = goldstein(jnp.pad(coherent, ((0, 0), (stride, stride), (stride, stride))))
        return (smoothed, magnitude)
    filtered, coherence = lax.map(one_slot, assignment)
    return (filtered, coherence)
```

```python
import functools
import math

import jax
import jax.numpy as jnp
import numpy as np
from jax import lax
from jax.experimental import pallas as pl
from jax.experimental.pallas import tpu as pltpu
from jax.sharding import PartitionSpec as P

PATCH = 32
LOOKS = 5
STRIDE = PATCH // 2
STRIP = 32
FLOOR = 1.0
TINY = 1e-06
GROUP = 2
f32 = jnp.float32
bf16 = jnp.bfloat16


def round_up(n, m):
    return (n + m - 1) // m * m


def halves(table):
    high = table.astype(bf16)
    low = (table - high.astype(np.float64)).astype(bf16)
    return high, low


def tables(height, width):
    index = np.arange(PATCH)
    angle = (index[:, None] * index[None, :] % PATCH) * (-2.0 * math.pi / PATCH)
    cos, sin = np.cos(angle), np.sin(angle)
    window = 1.0 - np.abs(index - (PATCH - 1) / 2.0) / STRIDE
    patch_rows, patch_cols = height // STRIDE + 1, width // STRIDE + 1
    half = round_up(patch_cols * PATCH, 128)
    rows = height + 2 * STRIDE
    first = np.zeros((2 * width + 128, 2 * half))
    for l in range(patch_cols):
        for j in range(PATCH):
            x = l * STRIDE - STRIDE + j
            if x < 0:
                real, imag = 2 * width + x + STRIDE, 2 * width + x + 3 * STRIDE
            elif x >= width:
                real, imag = 2 * width + STRIDE + x - width, 2 * width + 3 * STRIDE + x - width
            else:
                real, imag = x, width + x
            to = slice(l * PATCH, (l + 1) * PATCH)
            back = slice(half + l * PATCH, half + (l + 1) * PATCH)
            first[real, to] = cos[j]
            first[imag, to] = -sin[j]
            first[real, back] = sin[j]
            first[imag, back] = cos[j]
    upper = patch_rows * PATCH
    second = np.zeros((2 * upper, 2 * rows))
    fourth = np.zeros((2 * height, 2 * upper))
    for k in range(patch_rows):
        for i in range(PATCH):
            y = k * STRIDE - STRIDE + i
            row = y
            if y < 0:
                row = height + y + STRIDE
            elif y >= height:
                row = height + STRIDE + y - height
            to = slice(k * PATCH, (k + 1) * PATCH)
            back = slice(upper + k * PATCH, upper + (k + 1) * PATCH)
            second[to, row] = cos[i]
            second[to, rows + row] = -sin[i]
            second[back, row] = sin[i]
            second[back, rows + row] = cos[i]
            if 0 <= y < height:
                scale = window[i] / (PATCH * PATCH)
                fourth[y, to] += cos[i] * scale
                fourth[y, back] += sin[i] * scale
                fourth[height + y, to] += -sin[i] * scale
                fourth[height + y, back] += cos[i] * scale
    third = np.zeros((2 * half, 2 * width))
    for l in range(patch_cols):
        for j in range(PATCH):
            x = l * STRIDE - STRIDE + j
            if 0 <= x < width:
                to = slice(l * PATCH, (l + 1) * PATCH)
                back = slice(half + l * PATCH, half + (l + 1) * PATCH)
                third[to, x] += cos[j] * window[j]
                third[back, x] += sin[j] * window[j]
                third[to, width + x] += -sin[j] * window[j]
                third[back, width + x] += cos[j] * window[j]
    lane = np.arange(half)
    same = (lane[:, None] // PATCH == lane[None, :] // PATCH) / (PATCH * PATCH)
    same = same.astype(bf16)

    def right(table):
        high, low = halves(table)
        return np.concatenate([high, high, low], axis=0)

    def left(table):
        high, low = halves(table)
        return np.concatenate([high, high, low], axis=1)

    return right(first), left(second), np.concatenate([same, same], axis=0), right(third), left(fourth)


def split(x):
    high = x.astype(bf16)
    low = (x - high.astype(f32)).astype(bf16)
    return high, low


def dot(a, b):
    return jnp.dot(a, b, preferred_element_type=f32)


def body(jobs, slots, images, height, width, *refs):
    first_ref, second_ref, place_ref = refs[:3]
    tile_refs = refs[3 : 3 + images]
    box_rows, box_power, box_real, box_imag, w1, l2, ones, w3, l4 = refs[3 + images : 12 + images]
    out_filtered, out_coherence = refs[12 + images : 14 + images]
    cells, power, filtered, magnitude, sems = refs[14 + images :]
    rows = height + 2 * STRIDE
    half = w1.shape[1] // 2
    patch_rows = height // STRIDE + 1
    upper = patch_rows * PATCH

    def box(field, columns):
        high, low = split(field)
        tall = dot(box_rows[...], jnp.concatenate([high, low], axis=0))
        high, low = split(tall)
        return dot(jnp.concatenate([high, low], axis=1), columns[...])

    for i in range(images):
        real = tile_refs[i][0, 0].astype(f32)
        imag = tile_refs[i][0, 1].astype(f32)
        cells[i, 0] = real
        cells[i, 1] = imag
        power[i] = box(real * real + imag * imag, box_power)

    def stage(job):
        a, b = first_ref[job], second_ref[job]
        ur, ui, vr, vi = cells[a, 0], cells[a, 1], cells[b, 0], cells[b, 1]
        sum_real = box(ur * vr + ui * vi, box_real)
        sum_imag = box(ui * vr - ur * vi, box_imag)
        scale = lax.rsqrt(jnp.maximum(power[a] * power[b], FLOOR))
        own = scale[:, :width]
        c_real = sum_real[:, :width] * own
        c_imag = sum_imag[:, :width] * own
        c_halo = (sum_real[:, width:] + sum_imag[:, width:]) * scale[:, width:]
        m_real, m_imag = c_real[:height], c_imag[:height]
        magnitude[job] = jnp.sqrt(m_real * m_real + m_imag * m_imag)
        high, low = split(jnp.concatenate([c_real, c_imag, c_halo], axis=1))
        spec = dot(jnp.concatenate([high, low, high], axis=1), w1[...])
        high, low = split(jnp.concatenate([spec[:, :half], spec[:, half:]], axis=0))
        spec = dot(l2[...], jnp.concatenate([high, low, high], axis=0))
        z_real, z_imag = spec[:upper], spec[upper:]
        response = lax.rsqrt(lax.rsqrt(z_real * z_real + z_imag * z_imag))
        response = response.reshape(patch_rows, PATCH, half)
        sums = jnp.sum(response, axis=1)
        pad = round_up(patch_rows, 16) - patch_rows
        sums = jnp.concatenate([sums, jnp.zeros((pad, half), f32)], axis=0)
        high, low = split(sums)
        level = dot(jnp.concatenate([high, low], axis=1), ones[...]) + TINY
        inverse = (1.0 / level)[:patch_rows]
        weight = (response * inverse[:, None, :]).reshape(upper, half)
        high, low = split(jnp.concatenate([z_real * weight, z_imag * weight], axis=1))
        back = dot(jnp.concatenate([high, low, high], axis=1), w3[...])
        return jnp.concatenate([back[:, :width], back[:, width:]], axis=0)

    def copies(slot, job):
        return (
            pltpu.make_async_copy(filtered.at[job], out_filtered.at[slot], sems.at[0, slot]),
            pltpu.make_async_copy(magnitude.at[job], out_coherence.at[slot], sems.at[1, slot]),
        )

    def step(index, carry):
        start = index * GROUP
        backs = jnp.concatenate([stage(start + g) for g in range(GROUP)], axis=1)
        high, low = split(backs)
        result = dot(l4[...], jnp.concatenate([high, low, high], axis=0))
        for g in range(GROUP):
            part = result[:, g * width : (g + 1) * width]
            filtered[start + g, 0] = part[:height]
            filtered[start + g, 1] = part[height:]
        for slot in range(slots):
            job = place_ref[slot]

            @pl.when(jnp.logical_and(job >= start, job < start + GROUP))
            def _():
                for copy in copies(slot, job):
                    copy.start()

        return carry

    lax.fori_loop(0, jobs // GROUP, step, 0)
    for slot in range(slots):
        for copy in copies(slot, 0):
            copy.wait()


def strips(cells, axis, dim):
    count = lax.axis_size(axis)
    index = lax.axis_index(axis)
    extent = cells.shape[dim]
    head = lax.slice_in_dim(cells, 0, STRIP, axis=dim)
    tail = lax.slice_in_dim(cells, extent - STRIP, extent, axis=dim)
    step = jnp.arange(STRIP, dtype=jnp.int32)
    if count == 2:
        other = lax.ppermute(jnp.where(index == 0, tail, head), axis, [(0, 1), (1, 0)])
        return [other], [jnp.where(index == 0, extent, -STRIP) + step]
    before = lax.ppermute(tail, axis, [(i, i + 1) for i in range(count - 1)])
    after = lax.ppermute(head, axis, [(i + 1, i) for i in range(count - 1)])
    return [before, after], [step - STRIP, extent + step]


def banded(source, target, axis, extent):
    total = extent * lax.axis_size(axis)
    place = target + lax.axis_index(axis) * extent
    inside = (place >= 0) & (place < total)
    near = jnp.abs(source[:, None] - target[None, :]) <= LOOKS // 2
    return (near & inside[None, :]).astype(bf16)


FAR = 1 << 20


def on_device(slc_tiles, pair_list, assignment):
    height, width = slc_tiles.shape[2], slc_tiles.shape[3]
    acq = lax.axis_size("acq")
    me = lax.axis_index("acq")
    slots = assignment.shape[0] // acq
    side, side_places = strips(slc_tiles, "rg", 3)
    padding = jnp.zeros(slc_tiles.shape[:3] + (128 - STRIP * len(side),), bf16)
    tile = jnp.concatenate([slc_tiles, *side, padding], axis=3)
    ends, end_places = strips(tile, "az", 2)
    tile = jnp.concatenate([tile, *ends], axis=2)

    own_cols = jnp.arange(width, dtype=jnp.int32)
    own_rows = jnp.arange(height, dtype=jnp.int32)
    step = jnp.arange(STRIDE, dtype=jnp.int32)
    none = jnp.full((128,), FAR, jnp.int32)
    source_cols = jnp.concatenate([own_cols, *side_places, none[: 128 - STRIP * len(side)]])
    halo = jnp.concatenate([step - STRIDE, width + step])
    blank = none[: 2 * STRIDE]
    rest = none[: 128 - 4 * STRIDE]
    box_power = banded(source_cols, jnp.concatenate([own_cols, halo, halo, rest]), "rg", width)
    box_real = banded(source_cols, jnp.concatenate([own_cols, halo, blank, rest]), "rg", width)
    box_imag = banded(source_cols, jnp.concatenate([own_cols, blank, halo, rest]), "rg", width)
    source_rows = jnp.concatenate([own_rows, *end_places])
    target_rows = jnp.concatenate([own_rows, step - STRIDE, height + step])
    box_rows = banded(source_rows, target_rows, "az", height).T

    owned = lax.dynamic_slice_in_dim(assignment, me * slots, slots)
    pairs = jnp.take(pair_list, owned, axis=0)
    low, high = pairs[:, 0], pairs[:, 1]
    every = acq * (acq - 1) // 2
    if every <= slots:
        tiles = [tile]
        for k in range(1, acq):
            tiles.append(lax.ppermute(tile, "acq", [(i, (i + k) % acq) for i in range(acq)]))
        listed = [(a, b) for a in range(acq) for b in range(a + 1, acq)]
        jobs = every
        first = (me - jnp.array([a for a, _ in listed], jnp.int32)) % acq
        second = (me - jnp.array([b for _, b in listed], jnp.int32)) % acq
        place = low * acq - low * (low + 1) // 2 + high - low - 1
    else:
        gathered = lax.all_gather(tile, "acq", axis=0, tiled=True)
        tiles = [gathered[i : i + 1] for i in range(acq)]
        jobs, first, second = slots, low, high
        place = jnp.arange(slots, dtype=jnp.int32)
    return run(jobs, slots, height, width, first, second, place, tiles, (box_rows, box_power, box_real, box_imag))


def run(jobs, slots, height, width, first, second, place, tiles, boxes):
    images = len(tiles)
    box_rows, box_power, box_real, box_imag = boxes
    matrices = [
        jnp.concatenate([box_rows, box_rows], axis=1),
        jnp.concatenate([box_power, box_power], axis=0),
        jnp.concatenate([box_real, box_real], axis=0),
        jnp.concatenate([box_imag, box_imag], axis=0),
    ]
    matrices += [jnp.asarray(table) for table in tables(height, width)]
    smem = pl.BlockSpec(memory_space=pltpu.SMEM)
    vmem = pl.BlockSpec(memory_space=pltpu.VMEM)
    anywhere = pl.BlockSpec(memory_space=pl.ANY)
    rows = height + 2 * STRIDE
    return pl.pallas_call(
        functools.partial(body, jobs, slots, images, height, width),
        out_shape=(
            jax.ShapeDtypeStruct((slots, 2, height, width), f32),
            jax.ShapeDtypeStruct((slots, height, width), f32),
        ),
        in_specs=[smem] * 3 + [vmem] * (images + len(matrices)),
        out_specs=(anywhere, anywhere),
        scratch_shapes=[
            pltpu.VMEM((images, *tiles[0].shape[1:]), f32),
            pltpu.VMEM((images, rows, 2 * width), f32),
            pltpu.VMEM((jobs, 2, height, width), f32),
            pltpu.VMEM((jobs, height, width), f32),
            pltpu.SemaphoreType.DMA((2, slots)),
        ],
        compiler_params=pltpu.CompilerParams(vmem_limit_bytes=48 << 20),
    )(first, second, place, *tiles, *matrices)


def solution(mesh):
    return jax.shard_map(
        on_device,
        mesh=mesh,
        in_specs=(P("acq", None, ("groups", "az"), "rg"), P(), P()),
        out_specs=(P("acq", None, ("groups", "az"), "rg"), P("acq", ("groups", "az"), "rg")),
        check_vma=False,
    )
```
